32 devices in a mesh: seq: 2 (over x), ctx: 4 (over y, core), head: 4 (over z).
Axes of the slice: x: 2, y: 2, z: 4, core: 2. Of those that a mesh axis runs over, the one named last changes fastest.
Arguments:
- queries: bfloat16 [1536, 6144], P(('seq', 'ctx'), 'head'), parts along dimension 0, may hold values from -210 to 210
- kv_latent: bfloat16 [1536, 576], P(('seq', 'ctx')), parts along dimension 0, may hold values from -6 to 6
- kv_gain: float32 [512], replicated, may hold values from 0.25 to 1.75
- w_ukv: bfloat16 [512, 8192], P(None, 'head'), may hold values from -0.25 to 0.25
- w_out: bfloat16 [4096, 7168], P('head', 'ctx'), may hold values from -0.125 to 0.125
- row_position: int32 [1536], P('seq'), parts along dimension 0, may hold values from 0 to 767, as said below
Outputs:
- mixed: bfloat16 [1536, 7168], P(('seq', 'ctx'), 'head'), parts along dimension 0
The draws below stay inside these ranges and needn't reach their ends.
There are 2 independent parts, one for each index of `seq`. The reference program is written for one: setup_inputs(seed, part) draws one part's arguments, and reference() takes and returns one part's arrays. A program takes and returns all parts, laid end to end along the dimension named above; an argument that names none is the same for every part. Nothing has to cross between parts.
Inputs may be any that keep to these rules, and one draw needn't show every extreme that they name: `row_position`: the 768 values are a permutation of the positions. The rows of one index of ctx are two runs of 96 consecutive positions, the blocks b and 7 - b of the sequence cut into blocks of 96 positions, in either order.
All inputs are finite; a program needn't handle non-finite values.
Results may differ from the reference program's by a relative error of at most 0.012.
Values may be sent and summed in bfloat16 or wider, within the bound.
A program may use at most 128 MiB of HBM per device.

```python
import jax
import jax.numpy as jnp
from jax import lax

D = 7168
KVR = 512
NOPE = 128
ROPE = 64
VDIM = 128
HEAD_DEV = 8
TOK_DEV = 192
HEADS = 32
TOKENS = 768


def draw_queries(key, part):
    key = jax.random.fold_in(key, 3)
    shape = (TOKENS, HEADS * (NOPE + ROPE))
    return jax.random.truncated_normal(key, -4.0, 4.0, shape, jnp.float32).astype(jnp.bfloat16)


def draw_row_position(key, part):
    key = jax.random.fold_in(key, 7)
    count = TOKENS // TOK_DEV
    half = TOK_DEV // 2
    first, second = jax.random.split(key)
    lower = jax.random.permutation(first, count).astype(jnp.int32)
    flips = jax.random.randint(second, (count,), 0, 2)
    upper = 2 * count - 1 - lower
    leading = jnp.where(flips == 1, upper, lower)
    trailing = jnp.where(flips == 1, lower, upper)
    blocks = jnp.stack([leading, trailing], axis=1).reshape(-1)
    offsets = jnp.arange(half, dtype=jnp.int32)
    return (blocks[:, None] * half + offsets[None, :]).reshape(-1).astype(jnp.int32)


def with_spikes(result, own_key, source, target, parts, factor):
    owner, partner = [(jnp.arange(result.shape[position]) // (result.shape[position] // parts)).reshape([-1 if axis == position else 1 for axis in range(result.ndim)]) for position in (source, target)]
    chosen = jax.random.permutation(own_key, parts)[partner]
    strong = (owner == chosen) | (owner == (partner + parts // 2) % parts)
    return jnp.where(strong, factor * result, result)


def level_of(stream_key, dims, cuts, smallest, top_value):
    loudness = 1.0
    for axis_at, shards_of in cuts:
        heights = jax.random.uniform(jax.random.fold_in(jax.random.fold_in(stream_key, 6), axis_at), (shards_of,), jnp.float32, smallest / len(cuts), top_value / len(cuts))
        loudness = loudness * jnp.repeat(jnp.exp(heights), dims[axis_at] // shards_of).reshape((-1,) + (1,) * (len(dims) - 1 - axis_at))
    return loudness


def scatter_about(rng, dims, deviation, most, cuts=(), kind=jnp.bfloat16):
    factor_of = level_of(rng, dims, cuts, -0.22, 0.18) if cuts else 1.0
    values = jax.random.normal(rng, dims, jnp.float32) * deviation * factor_of
    return jnp.minimum(jnp.maximum(values, -most), most).astype(kind)


def heavy_noise(own_key, shape, deviation, reach, shards, heavy, kind=jnp.bfloat16):
    result = deviation * jax.random.normal(own_key, shape, jnp.float32)
    if shards:
        result = result * level_of(own_key, shape, shards, -0.22, 0.18)
    return jnp.clip(with_spikes(result, jax.random.fold_in(own_key, 3), *heavy), -reach, reach).astype(kind)


def setup_inputs(seed: int = 0, part: int = 0) -> dict:
    key_of = jax.random.split(jax.random.key(seed), 7)
    own_keys = jax.random.split(jax.random.fold_in(key_of[6], part), 7)
    queries = draw_queries(jax.random.fold_in(jax.random.fold_in(key_of[6], part), 71), part)
    kv_latent = scatter_about(own_keys[1], (TOKENS, KVR + ROPE), 1.0, 6.0, ((0, 4),))
    kv_gain = jnp.clip(1.0 + 0.15 * jax.random.normal(key_of[2], (KVR,), jnp.float32), 0.25, 1.75)
    w_ukv = scatter_about(key_of[3], (KVR, HEADS * (NOPE + VDIM)), KVR ** -0.5, 0.25, ((1, 4),))
    w_out = heavy_noise(key_of[4], (HEADS * VDIM, D), (HEADS * VDIM) ** -0.5, 0.125, ((0, 4), (1, 4)), (0, 1, 4, 2.0))
    row_position = draw_row_position(jax.random.fold_in(jax.random.fold_in(key_of[6], part), 71), part)
    return {"queries": queries, "kv_latent": kv_latent, "kv_gain": kv_gain, "w_ukv": w_ukv, "w_out": w_out, "row_position": row_position}


def reference(queries, kv_latent, kv_gain, w_ukv, w_out, row_position):
    rows = kv_latent.astype(jnp.float32)
    front = rows[:, :KVR]
    factor = lax.rsqrt(lax.optimization_barrier(jnp.mean(front * front, axis=1, keepdims=True)) + 1e-06)
    latent = jnp.concatenate([front * factor * kv_gain.astype(jnp.float32), rows[:, KVR:]], axis=1).astype(jnp.bfloat16)
    expanded = jnp.dot(latent[:, :KVR], w_ukv, preferred_element_type=jnp.float32).astype(jnp.bfloat16)
    expanded = jnp.transpose(expanded.reshape(TOKENS, HEADS, NOPE + VDIM), (1, 0, 2))
    q_heads = jnp.transpose(queries.reshape(TOKENS, HEADS, NOPE + ROPE), (1, 0, 2))
    rope_keys = latent[:, KVR:]
    allowed = row_position[None, :] <= row_position[:, None]
    factor_score = (NOPE + ROPE) ** (-0.5)

    def one_head(pair):
        q_head, e_head = pair
        key_head = e_head[:, :NOPE]
        value_head = e_head[:, NOPE:]
        keys = jnp.concatenate([key_head, rope_keys], axis=1)
        scores = jnp.dot(q_head, keys.T, preferred_element_type=jnp.float32) * factor_score
        scores = jnp.where(allowed, scores, -1e+30)
        peak = lax.optimization_barrier(jnp.max(scores, axis=1, keepdims=True))
        probs = jnp.where(allowed, jnp.exp(scores - peak), 0.0)
        total = lax.optimization_barrier(jnp.sum(probs, axis=1, keepdims=True))
        weights = probs.astype(jnp.bfloat16)
        summed = jnp.dot(weights, value_head, preferred_element_type=jnp.float32)
        return (summed / total).astype(jnp.bfloat16)
    heads_out = lax.map(one_head, (q_heads, expanded))
    attended = jnp.transpose(heads_out, (1, 0, 2)).reshape(TOKENS, HEADS * VDIM)
    groups = HEADS // HEAD_DEV
    group_rows = HEAD_DEV * VDIM
    att_groups = jnp.transpose(attended.reshape(TOKENS, groups, group_rows), (1, 0, 2))
    out_groups = w_out.reshape(groups, group_rows, D)

    def add_group(total, pair):
        att_part, out_part = pair
        partial_value = jnp.dot(att_part, out_part, preferred_element_type=jnp.float32).astype(jnp.bfloat16)
        return (total + partial_value.astype(jnp.float32), None)
    summed, unused = lax.scan(add_group, jnp.zeros((TOKENS, D), jnp.float32), (att_groups, out_groups))
    return summed.astype(jnp.bfloat16)
```

```python
import functools
import math

import jax
import jax.numpy as jnp
from jax import lax
from jax.experimental import pallas as pl
from jax.experimental.pallas import tpu as pltpu
from jax.sharding import PartitionSpec as P

KVR = 512
NOPE = 128
ROPE = 64
VDIM = 128
LAT = 640
CW = 256
F32 = jnp.float32
BF16 = jnp.bfloat16


def normalize(kv_latent, kv_gain):
    rows = kv_latent.astype(F32)
    front = rows[:, :KVR]
    factor = lax.rsqrt(jnp.mean(front * front, axis=1, keepdims=True) + 1e-06)
    return jnp.concatenate([front * factor * kv_gain, rows[:, KVR:]], axis=1).astype(BF16)


def layer_kernel(
    q_ref, kvl_ref, gain_ref, ukv_ref, own_pos_ref, key_pos_ref, wout_ref, out_ref,
    lat, keys, values, bias, att, w, pown, outbox, inbox,
    local_sem, lat_s, lat_r, core_s, core_r, y_s, y_r, x_s, x_r, cy_s, cy_r, cx_s, cx_r, ob_s, ib_r,
):
    x = lax.axis_index("seq")
    c = lax.axis_index("ctx")
    z = lax.axis_index("head")
    y = c // 2
    k = c % 2
    c_core = y * 2 + (1 - k)
    c_y = (1 - y) * 2 + k
    c_yc = (1 - y) * 2 + (1 - k)
    side = z // 2
    is_edge = (z % 2) == side
    partner = z + 1 - 2 * (z % 2)
    mid_far = 2 - side
    end_far = 3 * (1 - side)

    heads = values.shape[0]
    tok = q_ref.shape[0]
    depth, width = wout_ref.shape
    half = depth // 2
    chunks = width // CW
    qd = NOPE + ROPE

    core_id = (x, c_core, z)
    y_id = (x, c_y, z)
    x_id = (1 - x, c, z)

    barrier = pltpu.get_barrier_semaphore()
    for peer in (core_id, y_id, x_id, (x, c, partner), (x, c, mid_far), (x, c, end_far)):
        pl.semaphore_signal(barrier, inc=1, device_id=peer, device_id_type=pl.DeviceIdType.MESH)

    own_w = pltpu.make_async_copy(wout_ref, w.at[c], local_sem)
    own_w.start()

    raw = kvl_ref[...].astype(F32)
    front = raw[:, :KVR]
    factor = lax.rsqrt(jnp.mean(front * front, axis=1, keepdims=True) + 1e-06)
    lat[c, :, :KVR] = (front * factor * gain_ref[...]).astype(BF16)
    lat[c, :, KVR:] = jnp.concatenate(
        [kvl_ref[:, KVR:], jnp.zeros((tok, LAT - KVR - ROPE), BF16)], axis=1
    )
    pl.semaphore_wait(barrier, 6)

    def remote(src, dst, send, recv, dev):
        return pltpu.make_async_remote_copy(
            src_ref=src, dst_ref=dst, send_sem=send, recv_sem=recv,
            device_id=dev, device_id_type=pl.DeviceIdType.MESH,
        )

    def lat_copy(block, slot, dev):
        return remote(lat.at[block], lat.at[block], lat_s.at[slot], lat_r.at[slot], dev)

    lat_copy(c, 1, y_id).start()
    lat_copy(c, 0, core_id).start()
    own_to_core = remote(wout_ref, w.at[c], core_s, core_r, core_id)
    own_to_core.start()

    def part(block, which, n):
        rows = pl.ds(pl.multiple_of(which * half, half), half)
        return w.at[block, rows, pl.ds(pl.multiple_of(n * CW, CW), CW)]

    def y_copy(n):
        rows = pl.ds(pl.multiple_of(x * half, half), half)
        src = wout_ref.at[rows, pl.ds(pl.multiple_of(n * CW, CW), CW)]
        return remote(src, part(c, x, n), y_s.at[n], y_r.at[n], y_id)

    def y_in(n):
        return remote(part(c_y, x, n), part(c_y, x, n), y_s.at[n], y_r.at[n], y_id)

    def x_copy(n):
        return remote(part(c_y, x, n), part(c_y, x, n), x_s.at[n], x_r.at[n], x_id)

    def x_in(n):
        return remote(part(c_y, 1 - x, n), part(c_y, 1 - x, n), x_s.at[n], x_r.at[n], x_id)

    def cy_copy(n):
        return remote(part(c_y, x, n), part(c_y, x, n), cy_s.at[n], cy_r.at[n], core_id)

    def cy_in(n):
        return remote(part(c_yc, x, n), part(c_yc, x, n), cy_s.at[n], cy_r.at[n], core_id)

    def cx_copy(n):
        return remote(part(c_y, 1 - x, n), part(c_y, 1 - x, n), cx_s.at[n], cx_r.at[n], core_id)

    def cx_in(n):
        return remote(part(c_yc, 1 - x, n), part(c_yc, 1 - x, n), cx_s.at[n], cx_r.at[n], core_id)

    def pass_y(n):
        y_in(n).wait_recv()
        x_copy(n).start()
        cy_copy(n).start()

    def pass_x(n):
        x_in(n).wait_recv()
        cx_copy(n).start()

    def expand(block):
        rows = pl.ds(pl.multiple_of(block * tok, tok), tok)
        front = lat[block, :, :KVR]
        rope = lat[block, :, KVR:]
        for h in range(heads):
            cols = slice(h * (NOPE + VDIM), (h + 1) * (NOPE + VDIM))
            both = jnp.dot(front, ukv_ref[:, cols], preferred_element_type=F32).astype(BF16)
            keys[h, rows, :NOPE] = both[:, :NOPE]
            keys[h, rows, NOPE:] = rope
            values[h, rows, :] = both[:, NOPE:]

    expand(c)
    bias[...] = jnp.where(key_pos_ref[...] <= own_pos_ref[...], 0.0, -1e30).astype(F32)
    lat_copy(c_core, 0, core_id).wait_recv()
    expand(c_core)
    lat_copy(c_y, 1, y_id).wait_recv()
    lat_copy(c_y, 2, core_id).start()
    lat_copy(c, 1, y_id).wait_send()
    for n in range(chunks):
        y_copy(n).start()
    expand(c_y)
    lat_copy(c_yc, 2, core_id).wait_recv()
    expand(c_yc)

    scale = (NOPE + ROPE) ** (-0.5) * math.log2(math.e)
    for h in range(heads):
        q = q_ref[:, h * qd : (h + 1) * qd]
        q = jnp.concatenate([q, jnp.zeros((tok, 2 * NOPE - qd), BF16)], axis=1)
        scores = lax.dot_general(
            q, keys[h], (((1,), (1,)), ((), ())), preferred_element_type=F32
        )
        scores = scores * scale + bias[...]
        peak = jnp.max(scores, axis=1, keepdims=True)
        probs = jnp.exp2(scores - peak)
        total = jnp.sum(probs, axis=1, keepdims=True)
        summed = jnp.dot(probs.astype(BF16), values[h], preferred_element_type=F32)
        att[:, h * VDIM : (h + 1) * VDIM] = (summed / total).astype(BF16)

    pass_y(0)
    pass_y(1)
    pass_x(0)
    own_w.wait()
    own_to_core.wait_recv()

    def send(kind, n, slot, dev):
        return remote(
            outbox.at[kind, n], inbox.at[slot, n], ob_s.at[kind, n], ib_r.at[slot, n], (x, c, dev)
        )

    def arrived(slot, n):
        return remote(
            outbox.at[0, n], inbox.at[slot, n], ob_s.at[0, n], ib_r.at[slot, n], (x, c, partner)
        )

    def relay(n):
        for kind, dest in ((2, end_far), (1, mid_far)):
            arrived(1 + kind, n).wait_recv()
            outbox[kind, n] = (
                outbox[kind, n].astype(F32) + inbox[1 + kind, n].astype(F32)
            ).astype(BF16)
            send(kind, n, 1, dest).start()

    def step(n, carry):
        @pl.when(n + 2 < chunks)
        def _():
            pass_y(n + 2)

        @pl.when(n + 1 < chunks)
        def _():
            pass_x(n + 1)

        cy_in(n).wait_recv()
        cx_in(n).wait_recv()
        cols = pl.ds(pl.multiple_of(n * CW, CW), CW)

        def term(block):
            return jnp.dot(att[...], w[block, :, cols], preferred_element_type=F32)

        outbox[2, n] = term(end_far).astype(BF16)

        @pl.when(is_edge)
        def _():
            send(2, n, 3, partner).start()

        outbox[1, n] = term(mid_far).astype(BF16)

        @pl.when(is_edge)
        def _():
            send(1, n, 2, partner).start()

        outbox[0, n] = term(partner).astype(BF16)
        send(0, n, 0, partner).start()
        pown[n] = term(z)

        @pl.when(jnp.logical_and(jnp.logical_not(is_edge), n > 0))
        def _():
            relay(n - 1)

        return carry

    lax.fori_loop(0, chunks, step, 0)

    @pl.when(jnp.logical_not(is_edge))
    def _():
        relay(chunks - 1)

    for n in range(chunks):
        arrived(1, n).wait_recv()
        arrived(0, n).wait_recv()
        out_ref[:, n * CW : (n + 1) * CW] = (
            pown[n] + inbox[0, n].astype(F32) + inbox[1, n].astype(F32)
        ).astype(BF16)

    lat_copy(c, 0, core_id).wait_send()
    lat_copy(c_y, 2, core_id).wait_send()
    own_to_core.wait_send()

    def drain(n, carry):
        y_copy(n).wait_send()
        x_copy(n).wait_send()
        cy_copy(n).wait_send()
        cx_copy(n).wait_send()
        for kind in range(3):
            send(kind, n, 0, partner).wait_send()
        return carry

    lax.fori_loop(0, chunks, drain, 0)


def shards_fused(queries, kv_latent, kv_gain, w_ukv, w_out, row_position):
    tok = queries.shape[0]
    tokens = row_position.shape[0]
    heads = w_ukv.shape[1] // (NOPE + VDIM)
    depth, width = w_out.shape
    blocks = tokens // tok
    chunks = width // CW
    own_pos = lax.dynamic_slice_in_dim(row_position, lax.axis_index("ctx") * tok, tok)
    vmem = pl.BlockSpec(memory_space=pltpu.VMEM)
    dma = pltpu.SemaphoreType.DMA
    return pl.pallas_call(
        layer_kernel,
        out_shape=jax.ShapeDtypeStruct((tok, width), BF16),
        in_specs=[vmem] * 6 + [pl.BlockSpec(memory_space=pl.ANY)],
        out_specs=vmem,
        scratch_shapes=[
            pltpu.VMEM((blocks, tok, LAT), BF16),
            pltpu.VMEM((heads, tokens, 2 * NOPE), BF16),
            pltpu.VMEM((heads, tokens, VDIM), BF16),
            pltpu.VMEM((tok, tokens), F32),
            pltpu.VMEM((tok, heads * VDIM), BF16),
            pltpu.VMEM((blocks, depth, width), BF16),
            pltpu.VMEM((chunks, tok, CW), F32),
            pltpu.VMEM((3, chunks, tok, CW), BF16),
            pltpu.VMEM((4, chunks, tok, CW), BF16),
            dma,
            dma((3,)),
            dma((3,)),
            dma,
            dma,
        ]
        + [dma((chunks,))] * 8
        + [dma((3, chunks)), dma((4, chunks))],
        compiler_params=pltpu.CompilerParams(
            collective_id=0, has_side_effects=True, vmem_limit_bytes=56 * 1024 * 1024
        ),
        cost_estimate=pl.CostEstimate(
            flops=5_200_000_000, bytes_accessed=8_000_000, transcendentals=tok * tokens * heads
        ),
    )(
        queries, kv_latent, kv_gain.reshape(1, KVR), w_ukv, own_pos.reshape(tok, 1),
        row_position.reshape(1, tokens), w_out,
    )


def attend_piece(state, piece, key_pos, q_heads, own_pos, w_ukv):
    heads = q_heads.shape[1]
    length = piece.shape[0]
    factor_score = (NOPE + ROPE) ** (-0.5)
    for begin in range(0, length, 1024):
        size = min(1024, length - begin)
        rows = piece[begin : begin + size]
        positions = key_pos[begin : begin + size]
        peak, mass, acc = state
        expanded = jnp.dot(rows[:, :KVR], w_ukv, preferred_element_type=F32).astype(BF16)
        expanded = expanded.reshape(size, heads, NOPE + VDIM)
        scores = jnp.einsum(
            "qhd,khd->qhk", q_heads[:, :, :NOPE], expanded[:, :, :NOPE], preferred_element_type=F32
        )
        scores = scores + jnp.einsum(
            "qhd,kd->qhk", q_heads[:, :, NOPE:], rows[:, KVR:], preferred_element_type=F32
        )
        scores = scores * factor_score
        allowed = (positions[None, :] <= own_pos[:, None])[:, None, :]
        scores = jnp.where(allowed, scores, -1e30)
        new_peak = jnp.maximum(peak, jnp.max(scores, axis=2))
        shrink = jnp.exp(peak - new_peak)
        probs = jnp.where(allowed, jnp.exp(scores - new_peak[:, :, None]), 0.0)
        mass = mass * shrink + jnp.sum(probs, axis=2)
        added = jnp.einsum(
            "qhk,khd->qhd", probs.astype(BF16), expanded[:, :, NOPE:], preferred_element_type=F32
        )
        acc = acc * shrink[:, :, None] + added
        state = (new_peak, mass, acc)
    return state


def shards_general(queries, kv_latent, kv_gain, w_ukv, w_out, row_position):
    tok_rows = queries.shape[0]
    heads = w_ukv.shape[1] // (NOPE + VDIM)
    ctx_index = lax.axis_index("ctx")
    own_pos = lax.dynamic_slice_in_dim(row_position, ctx_index * tok_rows, tok_rows)
    latent = normalize(kv_latent, kv_gain)
    q_heads = queries.reshape(tok_rows, heads, NOPE + ROPE)
    start_state = (
        jnp.full((tok_rows, heads), -1e30, F32),
        jnp.zeros((tok_rows, heads), F32),
        jnp.zeros((tok_rows, heads, VDIM), F32),
    )
    every = lax.all_gather(latent, "ctx", axis=0, tiled=True)
    peak, mass, acc = attend_piece(start_state, every, row_position, q_heads, own_pos, w_ukv)
    attended = (acc / mass[:, :, None]).astype(BF16).reshape(tok_rows, heads * VDIM)
    terms = jnp.dot(
        attended, lax.all_gather(w_out, "ctx", axis=1, tiled=True), preferred_element_type=F32
    )
    return lax.psum_scatter(terms.astype(BF16), "head", scatter_dimension=1, tiled=True)


def solution(mesh):
    placed = (
        P(("seq", "ctx"), "head"),
        P(("seq", "ctx"), None),
        P(),
        P(None, "head"),
        P("head", "ctx"),
        P("seq"),
    )
    fused = (mesh.shape["seq"], mesh.shape["ctx"], mesh.shape["head"]) == (2, 4, 4)
    return jax.shard_map(
        shards_fused if fused else shards_general,
        mesh=mesh,
        in_specs=placed,
        out_specs=P(("seq", "ctx"), "head"),
        check_vma=False,
    )
```

```python
import functools
import math

import jax
import jax.numpy as jnp
from jax import lax
from jax.experimental import pallas as pl
from jax.experimental.pallas import tpu as pltpu
from jax.sharding import PartitionSpec as P

KVR = 512
NOPE = 128
ROPE = 64
VDIM = 128
LAT = 640
CW = 256
F32 = jnp.float32
BF16 = jnp.bfloat16


def normalize(kv_latent, kv_gain):
    rows = kv_latent.astype(F32)
    front = rows[:, :KVR]
    factor = lax.rsqrt(jnp.mean(front * front, axis=1, keepdims=True) + 1e-06)
    return jnp.concatenate([front * factor * kv_gain, rows[:, KVR:]], axis=1).astype(BF16)


def layer_kernel(
    kvl_ref, gain_ref, pos_ref, q_hbm, ukv_hbm, wout_ref, out_ref,
    q_ref, ukv_ref, lat, keys, values, bias, att, w, pown, outbox, inbox,
    local_sem, q_sem, ukv_sem, lat_s, lat_r, core_s, core_r, y_s, y_r, x_s, x_r, cy_s, cy_r, cx_s, cx_r, ob_s, ib_r,
):
    x = lax.axis_index("seq")
    c = lax.axis_index("ctx")
    z = lax.axis_index("head")
    y = c // 2
    k = c % 2
    c_core = y * 2 + (1 - k)
    c_y = (1 - y) * 2 + k
    c_yc = (1 - y) * 2 + (1 - k)
    side = z // 2
    is_edge = (z % 2) == side
    near_first = side == y
    partner = z + 1 - 2 * (z % 2)
    mid_far = 2 - side
    end_far = 3 * (1 - side)

    heads = values.shape[0]
    tok = q_ref.shape[0]
    depth, width = wout_ref.shape
    half = depth // 2
    chunks = width // CW
    qd = NOPE + ROPE

    core_id = (x, c_core, z)
    y_id = (x, c_y, z)
    x_id = (1 - x, c, z)

    barrier = pltpu.get_barrier_semaphore()
    for peer in (core_id, y_id, x_id, (x, c, partner), (x, c, mid_far), (x, c, end_far)):
        pl.semaphore_signal(barrier, inc=1, device_id=peer, device_id_type=pl.DeviceIdType.MESH)

    load_ukv = pltpu.make_async_copy(ukv_hbm, ukv_ref, ukv_sem)
    load_ukv.start()
    load_q = pltpu.make_async_copy(q_hbm, q_ref, q_sem)
    load_q.start()
    own_w = pltpu.make_async_copy(wout_ref, w.at[c], local_sem)
    own_w.start()

    raw = kvl_ref[...].astype(F32)
    front = raw[:, :KVR]
    factor = lax.rsqrt(jnp.mean(front * front, axis=1, keepdims=True) + 1e-06)
    lat[c, :, :KVR] = (front * factor * gain_ref[...].reshape(1, KVR)).astype(BF16)
    lat[c, :, KVR:] = jnp.concatenate(
        [kvl_ref[:, KVR:], jnp.zeros((tok, LAT - KVR - ROPE), BF16)], axis=1
    )
    pl.semaphore_wait(barrier, 6)

    def remote(src, dst, send, recv, dev):
        return pltpu.make_async_remote_copy(
            src_ref=src, dst_ref=dst, send_sem=send, recv_sem=recv,
            device_id=dev, device_id_type=pl.DeviceIdType.MESH,
        )

    def lat_copy(block, slot, dev):
        return remote(lat.at[block], lat.at[block], lat_s.at[slot], lat_r.at[slot], dev)

    lat_copy(c, 1, y_id).start()
    lat_copy(c, 0, core_id).start()
    own_to_core = remote(wout_ref, w.at[c], core_s, core_r, core_id)

    def part(block, which, n):
        rows = pl.ds(pl.multiple_of(which * half, half), half)
        return w.at[block, rows, pl.ds(pl.multiple_of(n * CW, CW), CW)]

    def y_copy(n):
        rows = pl.ds(pl.multiple_of(x * half, half), half)
        src = wout_ref.at[rows, pl.ds(pl.multiple_of(n * CW, CW), CW)]
        return remote(src, part(c, x, n), y_s.at[n], y_r.at[n], y_id)

    def y_in(n):
        return remote(part(c_y, x, n), part(c_y, x, n), y_s.at[n], y_r.at[n], y_id)

    def x_copy(n):
        return remote(part(c_y, x, n), part(c_y, x, n), x_s.at[n], x_r.at[n], x_id)

    def x_in(n):
        return remote(part(c_y, 1 - x, n), part(c_y, 1 - x, n), x_s.at[n], x_r.at[n], x_id)

    def cy_copy(n):
        return remote(part(c_y, x, n), part(c_y, x, n), cy_s.at[n], cy_r.at[n], core_id)

    def cy_in(n):
        return remote(part(c_yc, x, n), part(c_yc, x, n), cy_s.at[n], cy_r.at[n], core_id)

    def cx_copy(n):
        return remote(part(c_y, 1 - x, n), part(c_y, 1 - x, n), cx_s.at[n], cx_r.at[n], core_id)

    def cx_in(n):
        return remote(part(c_yc, 1 - x, n), part(c_yc, 1 - x, n), cx_s.at[n], cx_r.at[n], core_id)

    def pass_y(n):
        y_in(n).wait_recv()
        x_copy(n).start()
        cy_copy(n).start()

    def pass_x(n):
        x_in(n).wait_recv()
        cx_copy(n).start()

    def expand(block):
        rows = pl.ds(pl.multiple_of(block * tok, tok), tok)
        front = lat[block, :, :KVR]
        rope = lat[block, :, KVR:]
        for h in range(heads):
            cols = slice(h * (NOPE + VDIM), (h + 1) * (NOPE + VDIM))
            both = jnp.dot(front, ukv_ref[:, cols], preferred_element_type=F32).astype(BF16)
            keys[h, rows, :NOPE] = both[:, :NOPE]
            keys[h, rows, NOPE:] = rope
            values[h, rows, :] = both[:, NOPE:]

    for n in range(chunks):
        y_copy(n).start()
    own_to_core.start()

    key_pos = pos_ref[...].astype(F32).reshape(1, pos_ref.shape[0])
    shape = bias.shape
    own_row = lax.broadcasted_iota(jnp.int32, shape, 0) + c * tok
    is_own = lax.broadcasted_iota(jnp.int32, shape, 1) == own_row
    own_pos = jnp.sum(jnp.where(is_own, key_pos, 0.0), axis=1, keepdims=True)
    bias[...] = jnp.where(key_pos <= own_pos, 0.0, -1e30).astype(F32)
    load_ukv.wait()
    expand(c)
    lat_copy(c_core, 0, core_id).wait_recv()
    expand(c_core)
    lat_copy(c_y, 1, y_id).wait_recv()
    lat_copy(c_y, 2, core_id).start()
    expand(c_y)
    lat_copy(c_yc, 2, core_id).wait_recv()
    expand(c_yc)
    load_q.wait()

    scale = (NOPE + ROPE) ** (-0.5) * math.log2(math.e)
    for h in range(heads):
        q = q_ref[:, h * qd : (h + 1) * qd]
        q = jnp.concatenate([q, jnp.zeros((tok, 2 * NOPE - qd), BF16)], axis=1)
        scores = lax.dot_general(
            q, keys[h], (((1,), (1,)), ((), ())), preferred_element_type=F32
        )
        scores = scores * scale + bias[...]
        peak = jnp.max(scores, axis=1, keepdims=True)
        probs = jnp.exp2(scores - peak)
        total = jnp.sum(probs, axis=1, keepdims=True)
        summed = jnp.dot(probs.astype(BF16), values[h], preferred_element_type=F32)
        att[:, h * VDIM : (h + 1) * VDIM] = (summed / total).astype(BF16)
        if h == heads // 2:
            pass_y(0)

    own_w.wait()
    own_to_core.wait_recv()

    def send(kind, n, slot, dev):
        return remote(
            outbox.at[kind, n], inbox.at[slot, n], ob_s.at[kind, n], ib_r.at[slot, n], (x, c, dev)
        )

    def arrived(slot, n):
        return remote(
            outbox.at[0, n], inbox.at[slot, n], ob_s.at[0, n], ib_r.at[slot, n], (x, c, partner)
        )

    def relay(n):
        for kind, dest in ((2, end_far), (1, mid_far)):
            arrived(1 + kind, n).wait_recv()
            outbox[kind, n] = (
                outbox[kind, n].astype(F32) + inbox[1 + kind, n].astype(F32)
            ).astype(BF16)
            send(kind, n, 1, dest).start()

    def term(block, n):
        cols = pl.ds(pl.multiple_of(n * CW, CW), CW)
        return jnp.dot(att[...], w[block, :, cols], preferred_element_type=F32)

    def near(n):
        outbox[0, n] = term(partner, n).astype(BF16)
        send(0, n, 0, partner).start()
        pown[n] = term(z, n)

    def far(n):
        for kind, dest in ((2, end_far), (1, mid_far)):
            outbox[kind, n] = term(dest, n).astype(BF16)

            @pl.when(is_edge)
            def _():
                send(kind, n, 1 + kind, partner).start()

    def first(n, carry):
        @pl.when(near_first)
        def _():
            near(n)

        @pl.when(jnp.logical_not(near_first))
        def _():
            far(n)

        return carry

    def second(n, carry):
        @pl.when(n + 2 < chunks)
        def _():
            pass_y(n + 2)

        @pl.when(n + 1 < chunks)
        def _():
            pass_x(n + 1)

        cy_in(n).wait_recv()
        cx_in(n).wait_recv()

        @pl.when(near_first)
        def _():
            far(n)

        @pl.when(jnp.logical_not(near_first))
        def _():
            near(n)

        @pl.when(jnp.logical_and(jnp.logical_not(is_edge), n > 1))
        def _():
            relay(n - 2)

        return carry

    lax.fori_loop(0, chunks, first, 0)
    pass_y(1)
    pass_x(0)
    lax.fori_loop(0, chunks, second, 0)

    @pl.when(jnp.logical_not(is_edge))
    def _():
        relay(chunks - 2)
        relay(chunks - 1)

    for n in range(chunks):
        arrived(1, n).wait_recv()
        arrived(0, n).wait_recv()
        out_ref[:, n * CW : (n + 1) * CW] = (
            pown[n] + inbox[0, n].astype(F32) + inbox[1, n].astype(F32)
        ).astype(BF16)

    lat_copy(c, 0, core_id).wait_send()
    lat_copy(c, 1, y_id).wait_send()
    lat_copy(c_y, 2, core_id).wait_send()
    own_to_core.wait_send()

    def drain(n, carry):
        y_copy(n).wait_send()
        x_copy(n).wait_send()
        cy_copy(n).wait_send()
        cx_copy(n).wait_send()
        for kind in range(3):
            send(kind, n, 0, partner).wait_send()
        return carry

    lax.fori_loop(0, chunks, drain, 0)


def shards_fused(queries, kv_latent, kv_gain, w_ukv, w_out, row_position):
    tok = queries.shape[0]
    tokens = row_position.shape[0]
    heads = w_ukv.shape[1] // (NOPE + VDIM)
    depth, width = w_out.shape
    blocks = tokens // tok
    chunks = width // CW
    vmem = pl.BlockSpec(memory_space=pltpu.VMEM)
    dma = pltpu.SemaphoreType.DMA
    return pl.pallas_call(
        layer_kernel,
        out_shape=jax.ShapeDtypeStruct((tok, width), BF16),
        in_specs=[vmem] * 3 + [pl.BlockSpec(memory_space=pl.ANY)] * 3,
        out_specs=vmem,
        scratch_shapes=[
            pltpu.VMEM(queries.shape, BF16),
            pltpu.VMEM(w_ukv.shape, BF16),
            pltpu.VMEM((blocks, tok, LAT), BF16),
            pltpu.VMEM((heads, tokens, 2 * NOPE), BF16),
            pltpu.VMEM((heads, tokens, VDIM), BF16),
            pltpu.VMEM((tok, tokens), F32),
            pltpu.VMEM((tok, heads * VDIM), BF16),
            pltpu.VMEM((blocks, depth, width), BF16),
            pltpu.VMEM((chunks, tok, CW), F32),
            pltpu.VMEM((3, chunks, tok, CW), BF16),
            pltpu.VMEM((4, chunks, tok, CW), BF16),
            dma,
            dma,
            dma,
            dma((3,)),
            dma((3,)),
            dma,
            dma,
        ]
        + [dma((chunks,))] * 8
        + [dma((3, chunks)), dma((4, chunks))],
        compiler_params=pltpu.CompilerParams(
            collective_id=0, has_side_effects=True, vmem_limit_bytes=56 * 1024 * 1024
        ),
        cost_estimate=pl.CostEstimate(
            flops=5_200_000_000, bytes_accessed=8_000_000, transcendentals=tok * tokens * heads
        ),
    )(kv_latent, kv_gain, row_position, queries, w_ukv, w_out)


def attend_piece(state, piece, key_pos, q_heads, own_pos, w_ukv):
    heads = q_heads.shape[1]
    length = piece.shape[0]
    factor_score = (NOPE + ROPE) ** (-0.5)
    for begin in range(0, length, 1024):
        size = min(1024, length - begin)
        rows = piece[begin : begin + size]
        positions = key_pos[begin : begin + size]
        peak, mass, acc = state
        expanded = jnp.dot(rows[:, :KVR], w_ukv, preferred_element_type=F32).astype(BF16)
        expanded = expanded.reshape(size, heads, NOPE + VDIM)
        scores = jnp.einsum(
            "qhd,khd->qhk", q_heads[:, :, :NOPE], expanded[:, :, :NOPE], preferred_element_type=F32
        )
        scores = scores + jnp.einsum(
            "qhd,kd->qhk", q_heads[:, :, NOPE:], rows[:, KVR:], preferred_element_type=F32
        )
        scores = scores * factor_score
        allowed = (positions[None, :] <= own_pos[:, None])[:, None, :]
        scores = jnp.where(allowed, scores, -1e30)
        new_peak = jnp.maximum(peak, jnp.max(scores, axis=2))
        shrink = jnp.exp(peak - new_peak)
        probs = jnp.where(allowed, jnp.exp(scores - new_peak[:, :, None]), 0.0)
        mass = mass * shrink + jnp.sum(probs, axis=2)
        added = jnp.einsum(
            "qhk,khd->qhd", probs.astype(BF16), expanded[:, :, NOPE:], preferred_element_type=F32
        )
        acc = acc * shrink[:, :, None] + added
        state = (new_peak, mass, acc)
    return state


def shards_general(queries, kv_latent, kv_gain, w_ukv, w_out, row_position):
    tok_rows = queries.shape[0]
    heads = w_ukv.shape[1] // (NOPE + VDIM)
    ctx_index = lax.axis_index("ctx")
    own_pos = lax.dynamic_slice_in_dim(row_position, ctx_index * tok_rows, tok_rows)
    latent = normalize(kv_latent, kv_gain)
    q_heads = queries.reshape(tok_rows, heads, NOPE + ROPE)
    start_state = (
        jnp.full((tok_rows, heads), -1e30, F32),
        jnp.zeros((tok_rows, heads), F32),
        jnp.zeros((tok_rows, heads, VDIM), F32),
    )
    every = lax.all_gather(latent, "ctx", axis=0, tiled=True)
    peak, mass, acc = attend_piece(start_state, every, row_position, q_heads, own_pos, w_ukv)
    attended = (acc / mass[:, :, None]).astype(BF16).reshape(tok_rows, heads * VDIM)
    terms = jnp.dot(
        attended, lax.all_gather(w_out, "ctx", axis=1, tiled=True), preferred_element_type=F32
    )
    return lax.psum_scatter(terms.astype(BF16), "head", scatter_dimension=1, tiled=True)


def solution(mesh):
    placed = (
        P(("seq", "ctx"), "head"),
        P(("seq", "ctx"), None),
        P(),
        P(None, "head"),
        P("head", "ctx"),
        P("seq"),
    )
    fused = (mesh.shape["seq"], mesh.shape["ctx"], mesh.shape["head"]) == (2, 4, 4)
    return jax.shard_map(
        shards_fused if fused else shards_general,
        mesh=mesh,
        in_specs=placed,
        out_specs=P(("seq", "ctx"), "head"),
        check_vma=False,
    )
```

```python
import functools
import math

import jax
import jax.numpy as jnp
from jax import lax
from jax.experimental import pallas as pl
from jax.experimental.pallas import tpu as pltpu
from jax.sharding import PartitionSpec as P

KVR = 512
NOPE = 128
ROPE = 64
VDIM = 128
LAT = 640
CW = 128
EARLY = 3
F32 = jnp.float32
BF16 = jnp.bfloat16


def normalize(kv_latent, kv_gain):
    rows = kv_latent.astype(F32)
    front = rows[:, :KVR]
    factor = lax.rsqrt(jnp.mean(front * front, axis=1, keepdims=True) + 1e-06)
    return jnp.concatenate([front * factor * kv_gain, rows[:, KVR:]], axis=1).astype(BF16)


def layer_kernel(
    kvl_ref, gain_ref, pos_ref, q_hbm, ukv_hbm, wout_ref, out_ref,
    q_ref, ukv_ref, lat, keys, values, bias, att, w, pown, outbox, inbox,
    local_sem, q_sem, ukv_sem, lat_s, lat_r, core_s, core_r, y_s, y_r, x_s, x_r, cy_s, cy_r, cx_s, cx_r, ob_s, ib_r,
):
    x = lax.axis_index("seq")
    c = lax.axis_index("ctx")
    z = lax.axis_index("head")
    y = c // 2
    k = c % 2
    c_core = y * 2 + (1 - k)
    c_y = (1 - y) * 2 + k
    c_yc = (1 - y) * 2 + (1 - k)
    side = z // 2
    is_edge = (z % 2) == side
    near_first = side == y
    hold = jnp.logical_and(is_edge, near_first)
    partner = z + 1 - 2 * (z % 2)
    mid_far = 2 - side
    end_far = 3 * (1 - side)

    heads = values.shape[0]
    tok = q_ref.shape[0]
    depth, width = wout_ref.shape
    half = depth // 2
    chunks = width // CW
    qd = NOPE + ROPE

    core_id = (x, c_core, z)
    y_id = (x, c_y, z)
    x_id = (1 - x, c, z)

    barrier = pltpu.get_barrier_semaphore()
    for peer in (core_id, y_id, x_id, (x, c, partner), (x, c, mid_far), (x, c, end_far)):
        pl.semaphore_signal(barrier, inc=1, device_id=peer, device_id_type=pl.DeviceIdType.MESH)

    load_ukv = pltpu.make_async_copy(ukv_hbm, ukv_ref, ukv_sem)
    load_ukv.start()
    load_q = pltpu.make_async_copy(q_hbm, q_ref, q_sem)
    load_q.start()
    own_w = pltpu.make_async_copy(wout_ref, w.at[c], local_sem)

    raw = kvl_ref[...].astype(F32)
    front = raw[:, :KVR]
    factor = lax.rsqrt(jnp.mean(front * front, axis=1, keepdims=True) + 1e-06)
    lat[c, :, :KVR] = (front * factor * gain_ref[...].reshape(1, KVR)).astype(BF16)
    lat[c, :, KVR:] = jnp.concatenate(
        [kvl_ref[:, KVR:], jnp.zeros((tok, LAT - KVR - ROPE), BF16)], axis=1
    )
    pl.semaphore_wait(barrier, 6)

    def remote(src, dst, send, recv, dev):
        return pltpu.make_async_remote_copy(
            src_ref=src, dst_ref=dst, send_sem=send, recv_sem=recv,
            device_id=dev, device_id_type=pl.DeviceIdType.MESH,
        )

    def lat_copy(block, slot, dev):
        return remote(lat.at[block], lat.at[block], lat_s.at[slot], lat_r.at[slot], dev)

    lat_copy(c, 1, y_id).start()
    lat_copy(c, 0, core_id).start()
    own_to_core = remote(wout_ref, w.at[c], core_s, core_r, core_id)

    def part(block, which, n):
        rows = pl.ds(pl.multiple_of(which * half, half), half)
        return w.at[block, rows, pl.ds(pl.multiple_of(n * CW, CW), CW)]

    def y_copy(n):
        rows = pl.ds(pl.multiple_of(x * half, half), half)
        src = wout_ref.at[rows, pl.ds(pl.multiple_of(n * CW, CW), CW)]
        return remote(src, part(c, x, n), y_s.at[n], y_r.at[n], y_id)

    def y_in(n):
        return remote(part(c_y, x, n), part(c_y, x, n), y_s.at[n], y_r.at[n], y_id)

    def x_copy(n):
        return remote(part(c_y, x, n), part(c_y, x, n), x_s.at[n], x_r.at[n], x_id)

    def x_in(n):
        return remote(part(c_y, 1 - x, n), part(c_y, 1 - x, n), x_s.at[n], x_r.at[n], x_id)

    def cy_copy(n):
        return remote(part(c_y, x, n), part(c_y, x, n), cy_s.at[n], cy_r.at[n], core_id)

    def cy_in(n):
        return remote(part(c_yc, x, n), part(c_yc, x, n), cy_s.at[n], cy_r.at[n], core_id)

    def cx_copy(n):
        return remote(part(c_y, 1 - x, n), part(c_y, 1 - x, n), cx_s.at[n], cx_r.at[n], core_id)

    def cx_in(n):
        return remote(part(c_yc, 1 - x, n), part(c_yc, 1 - x, n), cx_s.at[n], cx_r.at[n], core_id)

    def pass_y(n):
        y_in(n).wait_recv()
        x_copy(n).start()
        cy_copy(n).start()

    def pass_x(n):
        x_in(n).wait_recv()
        cx_copy(n).start()

    def expand(block):
        rows = pl.ds(pl.multiple_of(block * tok, tok), tok)
        front = lat[block, :, :KVR]
        rope = lat[block, :, KVR:]
        for h in range(heads):
            cols = slice(h * (NOPE + VDIM), (h + 1) * (NOPE + VDIM))
            both = jnp.dot(front, ukv_ref[:, cols], preferred_element_type=F32).astype(BF16)
            keys[h, rows, :NOPE] = both[:, :NOPE]
            keys[h, rows, NOPE:] = rope
            values[h, rows, :] = both[:, NOPE:]

    for n in range(chunks):
        y_copy(n).start()
    own_to_core.start()
    own_w.start()

    key_pos = pos_ref[...].astype(F32).reshape(1, pos_ref.shape[0])
    shape = bias.shape
    own_row = lax.broadcasted_iota(jnp.int32, shape, 0) + c * tok
    is_own = lax.broadcasted_iota(jnp.int32, shape, 1) == own_row
    own_pos = jnp.sum(jnp.where(is_own, key_pos, 0.0), axis=1, keepdims=True)
    bias[...] = jnp.where(key_pos <= own_pos, 0.0, -1e30).astype(F32)
    load_ukv.wait()
    expand(c)
    lat_copy(c_core, 0, core_id).wait_recv()
    expand(c_core)
    lat_copy(c_y, 1, y_id).wait_recv()
    lat_copy(c_y, 2, core_id).start()
    expand(c_y)
    lat_copy(c_yc, 2, core_id).wait_recv()
    expand(c_yc)
    load_q.wait()

    scale = (NOPE + ROPE) ** (-0.5) * math.log2(math.e)
    for h in range(heads):
        q = q_ref[:, h * qd : (h + 1) * qd]
        q = jnp.concatenate([q, jnp.zeros((tok, 2 * NOPE - qd), BF16)], axis=1)
        scores = lax.dot_general(
            q, keys[h], (((1,), (1,)), ((), ())), preferred_element_type=F32
        )
        scores = scores * scale + bias[...]
        peak = jnp.max(scores, axis=1, keepdims=True)
        probs = jnp.exp2(scores - peak)
        total = jnp.sum(probs, axis=1, keepdims=True)
        summed = jnp.dot(probs.astype(BF16), values[h], preferred_element_type=F32)
        att[:, h * VDIM : (h + 1) * VDIM] = (summed / total).astype(BF16)
        if h == heads // 2:
            pass_y(0)

    own_w.wait()
    own_to_core.wait_recv()

    def send(kind, n, slot, dev):
        return remote(
            outbox.at[kind, n], inbox.at[slot, n], ob_s.at[kind, n], ib_r.at[slot, n], (x, c, dev)
        )

    def arrived(slot, n):
        return remote(
            outbox.at[0, n], inbox.at[slot, n], ob_s.at[0, n], ib_r.at[slot, n], (x, c, partner)
        )

    def relay(n):
        for kind, dest in ((2, end_far), (1, mid_far)):
            arrived(1 + kind, n).wait_recv()
            outbox[kind, n] = (
                outbox[kind, n].astype(F32) + inbox[1 + kind, n].astype(F32)
            ).astype(BF16)
            send(kind, n, 1, dest).start()

    def term(block, n):
        cols = pl.ds(pl.multiple_of(n * CW, CW), CW)
        return jnp.dot(att[...], w[block, :, cols], preferred_element_type=F32)

    def near(n):
        outbox[0, n] = term(partner, n).astype(BF16)

        @pl.when(jnp.logical_not(jnp.logical_and(hold, n >= EARLY)))
        def _():
            send(0, n, 0, partner).start()

        pown[n] = term(z, n)

    def far(n):
        for kind, dest in ((2, end_far), (1, mid_far)):
            outbox[kind, n] = term(dest, n).astype(BF16)

            @pl.when(is_edge)
            def _():
                send(kind, n, 1 + kind, partner).start()

    def first(n, carry):
        @pl.when(near_first)
        def _():
            near(n)

        @pl.when(jnp.logical_not(near_first))
        def _():
            far(n)

        return carry

    def second(n, carry):
        @pl.when(n + 2 < chunks)
        def _():
            pass_y(n + 2)

        @pl.when(n + 1 < chunks)
        def _():
            pass_x(n + 1)

        cy_in(n).wait_recv()
        cx_in(n).wait_recv()

        @pl.when(near_first)
        def _():
            far(n)

        @pl.when(jnp.logical_not(near_first))
        def _():
            near(n)

        @pl.when(jnp.logical_and(hold, n % 2 == 1))
        def _():
            send(0, EARLY + n // 2, 0, partner).start()

        @pl.when(jnp.logical_and(jnp.logical_not(is_edge), n > 0))
        def _():
            relay(n - 1)

        return carry

    lax.fori_loop(0, chunks, first, 0)
    pass_y(1)
    pass_x(0)
    lax.fori_loop(0, chunks, second, 0)

    @pl.when(jnp.logical_not(is_edge))
    def _():
        relay(chunks - 1)

    @pl.when(hold)
    def _():
        for n in range(EARLY + chunks // 2, chunks):
            send(0, n, 0, partner).start()

    for n in range(chunks):
        arrived(1, n).wait_recv()
        arrived(0, n).wait_recv()
        out_ref[:, n * CW : (n + 1) * CW] = (
            pown[n] + inbox[0, n].astype(F32) + inbox[1, n].astype(F32)
        ).astype(BF16)

    lat_copy(c, 0, core_id).wait_send()
    lat_copy(c, 1, y_id).wait_send()
    lat_copy(c_y, 2, core_id).wait_send()
    own_to_core.wait_send()

    def drain(n, carry):
        y_copy(n).wait_send()
        x_copy(n).wait_send()
        cy_copy(n).wait_send()
        cx_copy(n).wait_send()
        for kind in range(3):
            send(kind, n, 0, partner).wait_send()
        return carry

    lax.fori_loop(0, chunks, drain, 0)


def shards_fused(queries, kv_latent, kv_gain, w_ukv, w_out, row_position):
    tok = queries.shape[0]
    tokens = row_position.shape[0]
    heads = w_ukv.shape[1] // (NOPE + VDIM)
    depth, width = w_out.shape
    blocks = tokens // tok
    chunks = width // CW
    vmem = pl.BlockSpec(memory_space=pltpu.VMEM)
    dma = pltpu.SemaphoreType.DMA
    return pl.pallas_call(
        layer_kernel,
        out_shape=jax.ShapeDtypeStruct((tok, width), BF16),
        in_specs=[vmem] * 3 + [pl.BlockSpec(memory_space=pl.ANY)] * 3,
        out_specs=vmem,
        scratch_shapes=[
            pltpu.VMEM(queries.shape, BF16),
            pltpu.VMEM(w_ukv.shape, BF16),
            pltpu.VMEM((blocks, tok, LAT), BF16),
            pltpu.VMEM((heads, tokens, 2 * NOPE), BF16),
            pltpu.VMEM((heads, tokens, VDIM), BF16),
            pltpu.VMEM((tok, tokens), F32),
            pltpu.VMEM((tok, heads * VDIM), BF16),
            pltpu.VMEM((blocks, depth, width), BF16),
            pltpu.VMEM((chunks, tok, CW), F32),
            pltpu.VMEM((3, chunks, tok, CW), BF16),
            pltpu.VMEM((4, chunks, tok, CW), BF16),
            dma,
            dma,
            dma,
            dma((3,)),
            dma((3,)),
            dma,
            dma,
        ]
        + [dma((chunks,))] * 8
        + [dma((3, chunks)), dma((4, chunks))],
        compiler_params=pltpu.CompilerParams(
            collective_id=0, has_side_effects=True, vmem_limit_bytes=56 * 1024 * 1024
        ),
        cost_estimate=pl.CostEstimate(
            flops=5_200_000_000, bytes_accessed=8_000_000, transcendentals=tok * tokens * heads
        ),
    )(kv_latent, kv_gain, row_position, queries, w_ukv, w_out)


def attend_piece(state, piece, key_pos, q_heads, own_pos, w_ukv):
    heads = q_heads.shape[1]
    length = piece.shape[0]
    factor_score = (NOPE + ROPE) ** (-0.5)
    for begin in range(0, length, 1024):
        size = min(1024, length - begin)
        rows = piece[begin : begin + size]
        positions = key_pos[begin : begin + size]
        peak, mass, acc = state
        expanded = jnp.dot(rows[:, :KVR], w_ukv, preferred_element_type=F32).astype(BF16)
        expanded = expanded.reshape(size, heads, NOPE + VDIM)
        scores = jnp.einsum(
            "qhd,khd->qhk", q_heads[:, :, :NOPE], expanded[:, :, :NOPE], preferred_element_type=F32
        )
        scores = scores + jnp.einsum(
            "qhd,kd->qhk", q_heads[:, :, NOPE:], rows[:, KVR:], preferred_element_type=F32
        )
        scores = scores * factor_score
        allowed = (positions[None, :] <= own_pos[:, None])[:, None, :]
        scores = jnp.where(allowed, scores, -1e30)
        new_peak = jnp.maximum(peak, jnp.max(scores, axis=2))
        shrink = jnp.exp(peak - new_peak)
        probs = jnp.where(allowed, jnp.exp(scores - new_peak[:, :, None]), 0.0)
        mass = mass * shrink + jnp.sum(probs, axis=2)
        added = jnp.einsum(
            "qhk,khd->qhd", probs.astype(BF16), expanded[:, :, NOPE:], preferred_element_type=F32
        )
        acc = acc * shrink[:, :, None] + added
        state = (new_peak, mass, acc)
    return state


def shards_general(queries, kv_latent, kv_gain, w_ukv, w_out, row_position):
    tok_rows = queries.shape[0]
    heads = w_ukv.shape[1] // (NOPE + VDIM)
    ctx_index = lax.axis_index("ctx")
    own_pos = lax.dynamic_slice_in_dim(row_position, ctx_index * tok_rows, tok_rows)
    latent = normalize(kv_latent, kv_gain)
    q_heads = queries.reshape(tok_rows, heads, NOPE + ROPE)
    start_state = (
        jnp.full((tok_rows, heads), -1e30, F32),
        jnp.zeros((tok_rows, heads), F32),
        jnp.zeros((tok_rows, heads, VDIM), F32),
    )
    every = lax.all_gather(latent, "ctx", axis=0, tiled=True)
    peak, mass, acc = attend_piece(start_state, every, row_position, q_heads, own_pos, w_ukv)
    attended = (acc / mass[:, :, None]).astype(BF16).reshape(tok_rows, heads * VDIM)
    terms = jnp.dot(
        attended, lax.all_gather(w_out, "ctx", axis=1, tiled=True), preferred_element_type=F32
    )
    return lax.psum_scatter(terms.astype(BF16), "head", scatter_dimension=1, tiled=True)


def solution(mesh):
    placed = (
        P(("seq", "ctx"), "head"),
        P(("seq", "ctx"), None),
        P(),
        P(None, "head"),
        P("head", "ctx"),
        P("seq"),
    )
    fused = (mesh.shape["seq"], mesh.shape["ctx"], mesh.shape["head"]) == (2, 4, 4)
    return jax.shard_map(
        shards_fused if fused else shards_general,
        mesh=mesh,
        in_specs=placed,
        out_specs=P(("seq", "ctx"), "head"),
        check_vma=False,
    )
```

```python
import functools
import math

import jax
import jax.numpy as jnp
from jax import lax
from jax.experimental import pallas as pl
from jax.experimental.pallas import tpu as pltpu
from jax.sharding import PartitionSpec as P

KVR = 512
NOPE = 128
ROPE = 64
VDIM = 128
LAT = 640
CW = 256
F32 = jnp.float32
BF16 = jnp.bfloat16


def normalize(kv_latent, kv_gain):
    rows = kv_latent.astype(F32)
    front = rows[:, :KVR]
    factor = lax.rsqrt(jnp.mean(front * front, axis=1, keepdims=True) + 1e-06)
    return jnp.concatenate([front * factor * kv_gain, rows[:, KVR:]], axis=1).astype(BF16)


def layer_kernel(
    kvl_ref, gain_ref, pos_ref, q_hbm, ukv_hbm, wout_ref, out_ref,
    q_ref, ukv_ref, lat, keys, values, bias, att, w, pown, outbox, inbox,
    local_sem, q_sem, ukv_sem, lat_s, lat_r, core_s, core_r, y_s, y_r, x_s, x_r, cy_s, cy_r, cx_s, cx_r, ob_s, ib_r,
):
    x = lax.axis_index("seq")
    c = lax.axis_index("ctx")
    z = lax.axis_index("head")
    y = c // 2
    k = c % 2
    c_core = y * 2 + (1 - k)
    c_y = (1 - y) * 2 + k
    c_yc = (1 - y) * 2 + (1 - k)
    side = z // 2
    is_edge = (z % 2) == side
    near_first = side == y
    partner = z + 1 - 2 * (z % 2)
    mid_far = 2 - side
    end_far = 3 * (1 - side)

    heads = values.shape[0]
    tok = q_ref.shape[0]
    depth, width = wout_ref.shape
    half = depth // 2
    chunks = width // CW
    qd = NOPE + ROPE

    core_id = (x, c_core, z)
    y_id = (x, c_y, z)
    x_id = (1 - x, c, z)

    barrier = pltpu.get_barrier_semaphore()
    for peer in (core_id, y_id, x_id, (x, c, partner), (x, c, mid_far), (x, c, end_far)):
        pl.semaphore_signal(barrier, inc=1, device_id=peer, device_id_type=pl.DeviceIdType.MESH)

    load_ukv = pltpu.make_async_copy(ukv_hbm, ukv_ref, ukv_sem)
    load_ukv.start()
    load_q = pltpu.make_async_copy(q_hbm, q_ref, q_sem)
    load_q.start()
    own_w = pltpu.make_async_copy(wout_ref, w.at[c], local_sem)

    raw = kvl_ref[...].astype(F32)
    front = raw[:, :KVR]
    factor = lax.rsqrt(jnp.mean(front * front, axis=1, keepdims=True) + 1e-06)
    lat[c, :, :KVR] = (front * factor * gain_ref[...].reshape(1, KVR)).astype(BF16)
    lat[c, :, KVR:] = jnp.concatenate(
        [kvl_ref[:, KVR:], jnp.zeros((tok, LAT - KVR - ROPE), BF16)], axis=1
    )
    pl.semaphore_wait(barrier, 6)

    def remote(src, dst, send, recv, dev):
        return pltpu.make_async_remote_copy(
            src_ref=src, dst_ref=dst, send_sem=send, recv_sem=recv,
            device_id=dev, device_id_type=pl.DeviceIdType.MESH,
        )

    def lat_copy(block, slot, dev):
        return remote(lat.at[block], lat.at[block], lat_s.at[slot], lat_r.at[slot], dev)

    lat_copy(c, 1, y_id).start()
    lat_copy(c, 0, core_id).start()
    own_to_core = remote(wout_ref, w.at[c], core_s, core_r, core_id)

    def part(block, which, n):
        rows = pl.ds(pl.multiple_of(which * half, half), half)
        return w.at[block, rows, pl.ds(pl.multiple_of(n * CW, CW), CW)]

    def y_copy(n):
        rows = pl.ds(pl.multiple_of(x * half, half), half)
        src = wout_ref.at[rows, pl.ds(pl.multiple_of(n * CW, CW), CW)]
        return remote(src, part(c, x, n), y_s.at[n], y_r.at[n], y_id)

    def y_in(n):
        return remote(part(c_y, x, n), part(c_y, x, n), y_s.at[n], y_r.at[n], y_id)

    def x_copy(n):
        return remote(part(c_y, x, n), part(c_y, x, n), x_s.at[n], x_r.at[n], x_id)

    def x_in(n):
        return remote(part(c_y, 1 - x, n), part(c_y, 1 - x, n), x_s.at[n], x_r.at[n], x_id)

    def cy_copy(n):
        return remote(part(c_y, x, n), part(c_y, x, n), cy_s.at[n], cy_r.at[n], core_id)

    def cy_in(n):
        return remote(part(c_yc, x, n), part(c_yc, x, n), cy_s.at[n], cy_r.at[n], core_id)

    def cx_copy(n):
        return remote(part(c_y, 1 - x, n), part(c_y, 1 - x, n), cx_s.at[n], cx_r.at[n], core_id)

    def cx_in(n):
        return remote(part(c_yc, 1 - x, n), part(c_yc, 1 - x, n), cx_s.at[n], cx_r.at[n], core_id)

    def pass_y(n):
        y_in(n).wait_recv()
        x_copy(n).start()
        cy_copy(n).start()

    def pass_x(n):
        x_in(n).wait_recv()
        cx_copy(n).start()

    def expand(block):
        rows = pl.ds(pl.multiple_of(block * tok, tok), tok)
        front = lat[block, :, :KVR]
        rope = lat[block, :, KVR:]
        for h in range(heads):
            cols = slice(h * (NOPE + VDIM), (h + 1) * (NOPE + VDIM))
            both = jnp.dot(front, ukv_ref[:, cols], preferred_element_type=F32).astype(BF16)
            keys[h, rows, :NOPE] = both[:, :NOPE]
            keys[h, rows, NOPE:] = rope
            values[h, rows, :] = both[:, NOPE:]

    for n in range(chunks):
        y_copy(n).start()
    own_to_core.start()
    own_w.start()

    key_pos = pos_ref[...].astype(F32).reshape(1, pos_ref.shape[0])
    shape = bias.shape
    own_row = lax.broadcasted_iota(jnp.int32, shape, 0) + c * tok
    is_own = lax.broadcasted_iota(jnp.int32, shape, 1) == own_row
    own_pos = jnp.sum(jnp.where(is_own, key_pos, 0.0), axis=1, keepdims=True)
    bias[...] = jnp.where(key_pos <= own_pos, 0.0, -1e30).astype(F32)
    load_ukv.wait()
    expand(c)
    lat_copy(c_core, 0, core_id).wait_recv()
    expand(c_core)
    lat_copy(c_y, 1, y_id).wait_recv()
    lat_copy(c_y, 2, core_id).start()
    expand(c_y)
    lat_copy(c_yc, 2, core_id).wait_recv()
    expand(c_yc)
    load_q.wait()

    scale = (NOPE + ROPE) ** (-0.5) * math.log2(math.e)
    for h in range(heads):
        q = q_ref[:, h * qd : (h + 1) * qd]
        q = jnp.concatenate([q, jnp.zeros((tok, 2 * NOPE - qd), BF16)], axis=1)
        scores = lax.dot_general(
            q, keys[h], (((1,), (1,)), ((), ())), preferred_element_type=F32
        )
        scores = scores * scale + bias[...]
        peak = jnp.max(scores, axis=1, keepdims=True)
        probs = jnp.exp2(scores - peak)
        total = jnp.sum(probs, axis=1, keepdims=True)
        summed = jnp.dot(probs.astype(BF16), values[h], preferred_element_type=F32)
        att[:, h * VDIM : (h + 1) * VDIM] = (summed / total).astype(BF16)
        if h == heads // 2:
            pass_y(0)

    own_w.wait()
    own_to_core.wait_recv()

    def send(kind, n, slot, dev):
        return remote(
            outbox.at[kind, n], inbox.at[slot, n], ob_s.at[kind, n], ib_r.at[slot, n], (x, c, dev)
        )

    def arrived(slot, n):
        return remote(
            outbox.at[0, n], inbox.at[slot, n], ob_s.at[0, n], ib_r.at[slot, n], (x, c, partner)
        )

    def relay(n):
        for kind, dest in ((2, end_far), (1, mid_far)):
            arrived(1 + kind, n).wait_recv()
            outbox[kind, n] = (
                outbox[kind, n].astype(F32) + inbox[1 + kind, n].astype(F32)
            ).astype(BF16)
            send(kind, n, 1, dest).start()

    def term(block, n):
        cols = pl.ds(pl.multiple_of(n * CW, CW), CW)
        return jnp.dot(att[...], w[block, :, cols], preferred_element_type=F32)

    def near(n):
        outbox[0, n] = term(partner, n).astype(BF16)
        send(0, n, 0, partner).start()
        pown[n] = term(z, n)

    def far(n):
        for kind, dest in ((2, end_far), (1, mid_far)):
            outbox[kind, n] = term(dest, n).astype(BF16)

            @pl.when(is_edge)
            def _():
                send(kind, n, 1 + kind, partner).start()

    def first(n, carry):
        @pl.when(near_first)
        def _():
            near(n)

        @pl.when(jnp.logical_not(near_first))
        def _():
            far(n)

        return carry

    def second(n, carry):
        @pl.when(n + 2 < chunks)
        def _():
            pass_y(n + 2)

        @pl.when(n + 1 < chunks)
        def _():
            pass_x(n + 1)

        cy_in(n).wait_recv()
        cx_in(n).wait_recv()

        @pl.when(near_first)
        def _():
            far(n)

        @pl.when(jnp.logical_not(near_first))
        def _():
            near(n)

        @pl.when(jnp.logical_and(jnp.logical_not(is_edge), n > 0))
        def _():
            relay(n - 1)

        return carry

    lax.fori_loop(0, chunks, first, 0)
    pass_y(1)
    pass_x(0)
    lax.fori_loop(0, chunks, second, 0)

    @pl.when(jnp.logical_not(is_edge))
    def _():
        relay(chunks - 1)

    for n in range(chunks):
        arrived(1, n).wait_recv()
        arrived(0, n).wait_recv()
        out_ref[:, n * CW : (n + 1) * CW] = (
            pown[n] + inbox[0, n].astype(F32) + inbox[1, n].astype(F32)
        ).astype(BF16)

    lat_copy(c, 0, core_id).wait_send()
    lat_copy(c, 1, y_id).wait_send()
    lat_copy(c_y, 2, core_id).wait_send()
    own_to_core.wait_send()

    def drain(n, carry):
        y_copy(n).wait_send()
        x_copy(n).wait_send()
        cy_copy(n).wait_send()
        cx_copy(n).wait_send()
        for kind in range(3):
            send(kind, n, 0, partner).wait_send()
        return carry

    lax.fori_loop(0, chunks, drain, 0)


def shards_fused(queries, kv_latent, kv_gain, w_ukv, w_out, row_position):
    tok = queries.shape[0]
    tokens = row_position.shape[0]
    heads = w_ukv.shape[1] // (NOPE + VDIM)
    depth, width = w_out.shape
    blocks = tokens // tok
    chunks = width // CW
    vmem = pl.BlockSpec(memory_space=pltpu.VMEM)
    dma = pltpu.SemaphoreType.DMA
    return pl.pallas_call(
        layer_kernel,
        out_shape=jax.ShapeDtypeStruct((tok, width), BF16),
        in_specs=[vmem] * 3 + [pl.BlockSpec(memory_space=pl.ANY)] * 3,
        out_specs=vmem,
        scratch_shapes=[
            pltpu.VMEM(queries.shape, BF16),
            pltpu.VMEM(w_ukv.shape, BF16),
            pltpu.VMEM((blocks, tok, LAT), BF16),
            pltpu.VMEM((heads, tokens, 2 * NOPE), BF16),
            pltpu.VMEM((heads, tokens, VDIM), BF16),
            pltpu.VMEM((tok, tokens), F32),
            pltpu.VMEM((tok, heads * VDIM), BF16),
            pltpu.VMEM((blocks, depth, width), BF16),
            pltpu.VMEM((chunks, tok, CW), F32),
            pltpu.VMEM((3, chunks, tok, CW), BF16),
            pltpu.VMEM((4, chunks, tok, CW), BF16),
            dma,
            dma,
            dma,
            dma((3,)),
            dma((3,)),
            dma,
            dma,
        ]
        + [dma((chunks,))] * 8
        + [dma((3, chunks)), dma((4, chunks))],
        compiler_params=pltpu.CompilerParams(
            collective_id=0, has_side_effects=True, vmem_limit_bytes=56 * 1024 * 1024
        ),
        cost_estimate=pl.CostEstimate(
            flops=5_200_000_000, bytes_accessed=8_000_000, transcendentals=tok * tokens * heads
        ),
    )(kv_latent, kv_gain, row_position, queries, w_ukv, w_out)


def attend_piece(state, piece, key_pos, q_heads, own_pos, w_ukv):
    heads = q_heads.shape[1]
    length = piece.shape[0]
    factor_score = (NOPE + ROPE) ** (-0.5)
    for begin in range(0, length, 1024):
        size = min(1024, length - begin)
        rows = piece[begin : begin + size]
        positions = key_pos[begin : begin + size]
        peak, mass, acc = state
        expanded = jnp.dot(rows[:, :KVR], w_ukv, preferred_element_type=F32).astype(BF16)
        expanded = expanded.reshape(size, heads, NOPE + VDIM)
        scores = jnp.einsum(
            "qhd,khd->qhk", q_heads[:, :, :NOPE], expanded[:, :, :NOPE], preferred_element_type=F32
        )
        scores = scores + jnp.einsum(
            "qhd,kd->qhk", q_heads[:, :, NOPE:], rows[:, KVR:], preferred_element_type=F32
        )
        scores = scores * factor_score
        allowed = (positions[None, :] <= own_pos[:, None])[:, None, :]
        scores = jnp.where(allowed, scores, -1e30)
        new_peak = jnp.maximum(peak, jnp.max(scores, axis=2))
        shrink = jnp.exp(peak - new_peak)
        probs = jnp.where(allowed, jnp.exp(scores - new_peak[:, :, None]), 0.0)
        mass = mass * shrink + jnp.sum(probs, axis=2)
        added = jnp.einsum(
            "qhk,khd->qhd", probs.astype(BF16), expanded[:, :, NOPE:], preferred_element_type=F32
        )
        acc = acc * shrink[:, :, None] + added
        state = (new_peak, mass, acc)
    return state


def shards_general(queries, kv_latent, kv_gain, w_ukv, w_out, row_position):
    tok_rows = queries.shape[0]
    heads = w_ukv.shape[1] // (NOPE + VDIM)
    ctx_index = lax.axis_index("ctx")
    own_pos = lax.dynamic_slice_in_dim(row_position, ctx_index * tok_rows, tok_rows)
    latent = normalize(kv_latent, kv_gain)
    q_heads = queries.reshape(tok_rows, heads, NOPE + ROPE)
    start_state = (
        jnp.full((tok_rows, heads), -1e30, F32),
        jnp.zeros((tok_rows, heads), F32),
        jnp.zeros((tok_rows, heads, VDIM), F32),
    )
    every = lax.all_gather(latent, "ctx", axis=0, tiled=True)
    peak, mass, acc = attend_piece(start_state, every, row_position, q_heads, own_pos, w_ukv)
    attended = (acc / mass[:, :, None]).astype(BF16).reshape(tok_rows, heads * VDIM)
    terms = jnp.dot(
        attended, lax.all_gather(w_out, "ctx", axis=1, tiled=True), preferred_element_type=F32
    )
    return lax.psum_scatter(terms.astype(BF16), "head", scatter_dimension=1, tiled=True)


def solution(mesh):
    placed = (
        P(("seq", "ctx"), "head"),
        P(("seq", "ctx"), None),
        P(),
        P(None, "head"),
        P("head", "ctx"),
        P("seq"),
    )
    fused = (mesh.shape["seq"], mesh.shape["ctx"], mesh.shape["head"]) == (2, 4, 4)
    return jax.shard_map(
        shards_fused if fused else shards_general,
        mesh=mesh,
        in_specs=placed,
        out_specs=P(("seq", "ctx"), "head"),
        check_vma=False,
    )
```

```python
import functools
import math

import jax
import jax.numpy as jnp
from jax import lax
from jax.experimental import pallas as pl
from jax.experimental.pallas import tpu as pltpu
from jax.sharding import PartitionSpec as P

KVR = 512
NOPE = 128
ROPE = 64
VDIM = 128
LAT = 640
CW = 256
F32 = jnp.float32
BF16 = jnp.bfloat16


def normalize(kv_latent, kv_gain):
    rows = kv_latent.astype(F32)
    front = rows[:, :KVR]
    factor = lax.rsqrt(jnp.mean(front * front, axis=1, keepdims=True) + 1e-06)
    return jnp.concatenate([front * factor * kv_gain, rows[:, KVR:]], axis=1).astype(BF16)


def layer_kernel(
    kvl_ref, gain_ref, pos_ref, q_hbm, ukv_hbm, wout_ref, out_ref,
    q_ref, ukv_ref, lat, keys, values, bias, att, w, pown, outbox, inbox,
    local_sem, q_sem, ukv_sem, lat_s, lat_r, core_s, core_r, y_s, y_r, x_s, x_r, cy_s, cy_r, cx_s, cx_r, ob_s, ib_r,
):
    x = lax.axis_index("seq")
    c = lax.axis_index("ctx")
    z = lax.axis_index("head")
    y = c // 2
    k = c % 2
    c_core = y * 2 + (1 - k)
    c_y = (1 - y) * 2 + k
    c_yc = (1 - y) * 2 + (1 - k)
    side = z // 2
    is_edge = (z % 2) == side
    near_first = side == y
    partner = z + 1 - 2 * (z % 2)
    mid_far = 2 - side
    end_far = 3 * (1 - side)

    heads = values.shape[0]
    tok = q_ref.shape[0]
    depth, width = wout_ref.shape
    half = depth // 2
    chunks = width // CW
    qd = NOPE + ROPE

    core_id = (x, c_core, z)
    y_id = (x, c_y, z)
    x_id = (1 - x, c, z)

    barrier = pltpu.get_barrier_semaphore()
    for peer in (core_id, y_id, x_id, (x, c, partner), (x, c, mid_far), (x, c, end_far)):
        pl.semaphore_signal(barrier, inc=1, device_id=peer, device_id_type=pl.DeviceIdType.MESH)

    load_ukv = pltpu.make_async_copy(ukv_hbm, ukv_ref, ukv_sem)
    load_ukv.start()
    load_q = pltpu.make_async_copy(q_hbm, q_ref, q_sem)
    load_q.start()
    own_w = pltpu.make_async_copy(wout_ref, w.at[c], local_sem)

    raw = kvl_ref[...].astype(F32)
    front = raw[:, :KVR]
    factor = lax.rsqrt(jnp.mean(front * front, axis=1, keepdims=True) + 1e-06)
    lat[c, :, :KVR] = (front * factor * gain_ref[...].reshape(1, KVR)).astype(BF16)
    lat[c, :, KVR:] = jnp.concatenate(
        [kvl_ref[:, KVR:], jnp.zeros((tok, LAT - KVR - ROPE), BF16)], axis=1
    )
    pl.semaphore_wait(barrier, 6)

    def remote(src, dst, send, recv, dev):
        return pltpu.make_async_remote_copy(
            src_ref=src, dst_ref=dst, send_sem=send, recv_sem=recv,
            device_id=dev, device_id_type=pl.DeviceIdType.MESH,
        )

    def lat_copy(block, slot, dev):
        return remote(lat.at[block], lat.at[block], lat_s.at[slot], lat_r.at[slot], dev)

    lat_copy(c, 1, y_id).start()
    lat_copy(c, 0, core_id).start()
    own_to_core = remote(wout_ref, w.at[c], core_s, core_r, core_id)

    def part(block, which, n):
        rows = pl.ds(pl.multiple_of(which * half, half), half)
        return w.at[block, rows, pl.ds(pl.multiple_of(n * CW, CW), CW)]

    def y_copy(n):
        rows = pl.ds(pl.multiple_of(x * half, half), half)
        src = wout_ref.at[rows, pl.ds(pl.multiple_of(n * CW, CW), CW)]
        return remote(src, part(c, x, n), y_s.at[n], y_r.at[n], y_id)

    def y_in(n):
        return remote(part(c_y, x, n), part(c_y, x, n), y_s.at[n], y_r.at[n], y_id)

    def x_copy(n):
        return remote(part(c_y, x, n), part(c_y, x, n), x_s.at[n], x_r.at[n], x_id)

    def x_in(n):
        return remote(part(c_y, 1 - x, n), part(c_y, 1 - x, n), x_s.at[n], x_r.at[n], x_id)

    def cy_copy(n):
        return remote(part(c_y, x, n), part(c_y, x, n), cy_s.at[n], cy_r.at[n], core_id)

    def cy_in(n):
        return remote(part(c_yc, x, n), part(c_yc, x, n), cy_s.at[n], cy_r.at[n], core_id)

    def cx_copy(n):
        return remote(part(c_y, 1 - x, n), part(c_y, 1 - x, n), cx_s.at[n], cx_r.at[n], core_id)

    def cx_in(n):
        return remote(part(c_yc, 1 - x, n), part(c_yc, 1 - x, n), cx_s.at[n], cx_r.at[n], core_id)

    def pass_y(n):
        y_in(n).wait_recv()
        x_copy(n).start()
        cy_copy(n).start()

    def pass_x(n):
        x_in(n).wait_recv()
        cx_copy(n).start()

    def expand(block):
        rows = pl.ds(pl.multiple_of(block * tok, tok), tok)
        front = lat[block, :, :KVR]
        rope = lat[block, :, KVR:]
        for h in range(heads):
            cols = slice(h * (NOPE + VDIM), (h + 1) * (NOPE + VDIM))
            both = jnp.dot(front, ukv_ref[:, cols], preferred_element_type=F32).astype(BF16)
            keys[h, rows, :NOPE] = both[:, :NOPE]
            keys[h, rows, NOPE:] = rope
            values[h, rows, :] = both[:, NOPE:]

    for n in range(chunks):
        y_copy(n).start()
    own_to_core.start()
    own_w.start()

    key_pos = pos_ref[...].astype(F32).reshape(1, pos_ref.shape[0])
    shape = bias.shape
    own_row = lax.broadcasted_iota(jnp.int32, shape, 0) + c * tok
    is_own = lax.broadcasted_iota(jnp.int32, shape, 1) == own_row
    own_pos = jnp.sum(jnp.where(is_own, key_pos, 0.0), axis=1, keepdims=True)
    bias[...] = jnp.where(key_pos <= own_pos, 0.0, -1e30).astype(F32)
    load_ukv.wait()
    expand(c)
    lat_copy(c_core, 0, core_id).wait_recv()
    expand(c_core)
    lat_copy(c_y, 1, y_id).wait_recv()
    lat_copy(c_y, 2, core_id).start()
    expand(c_y)
    lat_copy(c_yc, 2, core_id).wait_recv()
    expand(c_yc)
    load_q.wait()

    scale = (NOPE + ROPE) ** (-0.5) * math.log2(math.e)
    for h in range(heads):
        q = q_ref[:, h * qd : (h + 1) * qd]
        q = jnp.concatenate([q, jnp.zeros((tok, 2 * NOPE - qd), BF16)], axis=1)
        scores = lax.dot_general(
            q, keys[h], (((1,), (1,)), ((), ())), preferred_element_type=F32
        )
        scores = scores * scale + bias[...]
        peak = jnp.max(scores, axis=1, keepdims=True)
        probs = jnp.exp2(scores - peak)
        total = jnp.sum(probs, axis=1, keepdims=True)
        summed = jnp.dot(probs.astype(BF16), values[h], preferred_element_type=F32)
        att[:, h * VDIM : (h + 1) * VDIM] = (summed / total).astype(BF16)
        if h == heads // 2:
            pass_y(0)

    own_w.wait()
    own_to_core.wait_recv()

    def send(kind, n, slot, dev):
        return remote(
            outbox.at[kind, n], inbox.at[slot, n], ob_s.at[kind, n], ib_r.at[slot, n], (x, c, dev)
        )

    def arrived(slot, n):
        return remote(
            outbox.at[0, n], inbox.at[slot, n], ob_s.at[0, n], ib_r.at[slot, n], (x, c, partner)
        )

    def relay(n):
        for kind, dest in ((2, end_far), (1, mid_far)):
            arrived(1 + kind, n).wait_recv()
            outbox[kind, n] = (
                outbox[kind, n].astype(F32) + inbox[1 + kind, n].astype(F32)
            ).astype(BF16)
            send(kind, n, 1, dest).start()

    def term(block, n):
        cols = pl.ds(pl.multiple_of(n * CW, CW), CW)
        return jnp.dot(att[...], w[block, :, cols], preferred_element_type=F32)

    def near(n):
        outbox[0, n] = term(partner, n).astype(BF16)
        send(0, n, 0, partner).start()
        pown[n] = term(z, n)

    def far(n):
        for kind, dest in ((2, end_far), (1, mid_far)):
            outbox[kind, n] = term(dest, n).astype(BF16)

            @pl.when(is_edge)
            def _():
                send(kind, n, 1 + kind, partner).start()

    def first(n, carry):
        @pl.when(near_first)
        def _():
            near(n)

        @pl.when(jnp.logical_not(near_first))
        def _():
            far(n)

        return carry

    middle = jnp.logical_not(is_edge)
    far_first = jnp.logical_not(near_first)

    def second(n, carry):
        @pl.when(middle & far_first & (n > 0))
        def _():
            relay(n - 1)

        @pl.when(middle & far_first & (n == chunks - 1))
        def _():
            relay(n)

        @pl.when(n + 2 < chunks)
        def _():
            pass_y(n + 2)

        @pl.when(n + 1 < chunks)
        def _():
            pass_x(n + 1)

        cy_in(n).wait_recv()
        cx_in(n).wait_recv()

        @pl.when(near_first)
        def _():
            far(n)

        @pl.when(jnp.logical_not(near_first))
        def _():
            near(n)

        @pl.when(middle & near_first & (n > 0))
        def _():
            relay(n - 1)

        return carry

    lax.fori_loop(0, chunks, first, 0)
    pass_y(1)
    pass_x(0)
    lax.fori_loop(0, chunks, second, 0)

    @pl.when(middle & near_first)
    def _():
        relay(chunks - 1)

    for n in range(chunks):
        arrived(1, n).wait_recv()
        arrived(0, n).wait_recv()
        out_ref[:, n * CW : (n + 1) * CW] = (
            pown[n] + inbox[0, n].astype(F32) + inbox[1, n].astype(F32)
        ).astype(BF16)

    lat_copy(c, 0, core_id).wait_send()
    lat_copy(c, 1, y_id).wait_send()
    lat_copy(c_y, 2, core_id).wait_send()
    own_to_core.wait_send()

    def drain(n, carry):
        y_copy(n).wait_send()
        x_copy(n).wait_send()
        cy_copy(n).wait_send()
        cx_copy(n).wait_send()
        for kind in range(3):
            send(kind, n, 0, partner).wait_send()
        return carry

    lax.fori_loop(0, chunks, drain, 0)


def shards_fused(queries, kv_latent, kv_gain, w_ukv, w_out, row_position):
    tok = queries.shape[0]
    tokens = row_position.shape[0]
    heads = w_ukv.shape[1] // (NOPE + VDIM)
    depth, width = w_out.shape
    blocks = tokens // tok
    chunks = width // CW
    vmem = pl.BlockSpec(memory_space=pltpu.VMEM)
    dma = pltpu.SemaphoreType.DMA
    return pl.pallas_call(
        layer_kernel,
        out_shape=jax.ShapeDtypeStruct((tok, width), BF16),
        in_specs=[vmem] * 3 + [pl.BlockSpec(memory_space=pl.ANY)] * 3,
        out_specs=vmem,
        scratch_shapes=[
            pltpu.VMEM(queries.shape, BF16),
            pltpu.VMEM(w_ukv.shape, BF16),
            pltpu.VMEM((blocks, tok, LAT), BF16),
            pltpu.VMEM((heads, tokens, 2 * NOPE), BF16),
            pltpu.VMEM((heads, tokens, VDIM), BF16),
            pltpu.VMEM((tok, tokens), F32),
            pltpu.VMEM((tok, heads * VDIM), BF16),
            pltpu.VMEM((blocks, depth, width), BF16),
            pltpu.VMEM((chunks, tok, CW), F32),
            pltpu.VMEM((3, chunks, tok, CW), BF16),
            pltpu.VMEM((4, chunks, tok, CW), BF16),
            dma,
            dma,
            dma,
            dma((3,)),
            dma((3,)),
            dma,
            dma,
        ]
        + [dma((chunks,))] * 8
        + [dma((3, chunks)), dma((4, chunks))],
        compiler_params=pltpu.CompilerParams(
            collective_id=0, has_side_effects=True, vmem_limit_bytes=56 * 1024 * 1024
        ),
        cost_estimate=pl.CostEstimate(
            flops=5_200_000_000, bytes_accessed=8_000_000, transcendentals=tok * tokens * heads
        ),
    )(kv_latent, kv_gain, row_position, queries, w_ukv, w_out)


def attend_piece(state, piece, key_pos, q_heads, own_pos, w_ukv):
    heads = q_heads.shape[1]
    length = piece.shape[0]
    factor_score = (NOPE + ROPE) ** (-0.5)
    for begin in range(0, length, 1024):
        size = min(1024, length - begin)
        rows = piece[begin : begin + size]
        positions = key_pos[begin : begin + size]
        peak, mass, acc = state
        expanded = jnp.dot(rows[:, :KVR], w_ukv, preferred_element_type=F32).astype(BF16)
        expanded = expanded.reshape(size, heads, NOPE + VDIM)
        scores = jnp.einsum(
            "qhd,khd->qhk", q_heads[:, :, :NOPE], expanded[:, :, :NOPE], preferred_element_type=F32
        )
        scores = scores + jnp.einsum(
            "qhd,kd->qhk", q_heads[:, :, NOPE:], rows[:, KVR:], preferred_element_type=F32
        )
        scores = scores * factor_score
        allowed = (positions[None, :] <= own_pos[:, None])[:, None, :]
        scores = jnp.where(allowed, scores, -1e30)
        new_peak = jnp.maximum(peak, jnp.max(scores, axis=2))
        shrink = jnp.exp(peak - new_peak)
        probs = jnp.where(allowed, jnp.exp(scores - new_peak[:, :, None]), 0.0)
        mass = mass * shrink + jnp.sum(probs, axis=2)
        added = jnp.einsum(
            "qhk,khd->qhd", probs.astype(BF16), expanded[:, :, NOPE:], preferred_element_type=F32
        )
        acc = acc * shrink[:, :, None] + added
        state = (new_peak, mass, acc)
    return state


def shards_general(queries, kv_latent, kv_gain, w_ukv, w_out, row_position):
    tok_rows = queries.shape[0]
    heads = w_ukv.shape[1] // (NOPE + VDIM)
    ctx_index = lax.axis_index("ctx")
    own_pos = lax.dynamic_slice_in_dim(row_position, ctx_index * tok_rows, tok_rows)
    latent = normalize(kv_latent, kv_gain)
    q_heads = queries.reshape(tok_rows, heads, NOPE + ROPE)
    start_state = (
        jnp.full((tok_rows, heads), -1e30, F32),
        jnp.zeros((tok_rows, heads), F32),
        jnp.zeros((tok_rows, heads, VDIM), F32),
    )
    every = lax.all_gather(latent, "ctx", axis=0, tiled=True)
    peak, mass, acc = attend_piece(start_state, every, row_position, q_heads, own_pos, w_ukv)
    attended = (acc / mass[:, :, None]).astype(BF16).reshape(tok_rows, heads * VDIM)
    terms = jnp.dot(
        attended, lax.all_gather(w_out, "ctx", axis=1, tiled=True), preferred_element_type=F32
    )
    return lax.psum_scatter(terms.astype(BF16), "head", scatter_dimension=1, tiled=True)


def solution(mesh):
    placed = (
        P(("seq", "ctx"), "head"),
        P(("seq", "ctx"), None),
        P(),
        P(None, "head"),
        P("head", "ctx"),
        P("seq"),
    )
    fused = (mesh.shape["seq"], mesh.shape["ctx"], mesh.shape["head"]) == (2, 4, 4)
    return jax.shard_map(
        shards_fused if fused else shards_general,
        mesh=mesh,
        in_specs=placed,
        out_specs=P(("seq", "ctx"), "head"),
        check_vma=False,
    )
```
